512 devices in a mesh: ga: 32 (over y_lo, z), band: 16 (over x, y_hi, core).
Axes of the slice: x: 4, y: 8 (y_hi: 2, y_lo: 4; y = y_hi * 4 + y_lo), z: 8, core: 2. Of those that a mesh axis runs over, the one named last changes fastest.
Arguments:
- becsum_part: float32 [16, 2048, 171], P('band'), may hold values from -0.03314563 to 0.03314563
- qrad: bfloat16 [2, 9, 128, 171], replicated, may hold values from -0.45703125 to 0.45703125
- positions: float32 [3, 2048], replicated, may hold values from 0 to 1
- species: int32 [2048], replicated, may hold values from 0 to 1
- miller: int32 [2, 512], P(None, 'ga'), may hold values from -192 to 191
Outputs:
- planes: float32 [2, 32, 16, 384], P(None, None, 'band', 'ga')
The draws below stay inside these ranges and needn't reach their ends.
All inputs are finite; a program needn't handle non-finite values.
Results may differ from the reference program's by a relative error of at most 0.0046.
Values sent between devices are 32-bit elements; how exact they have to be, the bound alone decides.
A program may use at most 64 MiB of HBM per device.

```python
import math
import jax
import jax.numpy as jnp
from jax import lax

NZ = 384
NIJ = 171
NQ = 128
NLM = 9
NSP = 2
NAT = 2048
COL_GA = 16
COLS = 512
N_GA = 32
N_BAND = 16


def with_ends(values, rng, low, largest):
    index_at = [jax.random.randint(jax.random.fold_in(rng, axis), (), 0, length) for axis, length in enumerate(values.shape)]
    widest = values.shape.index(max(values.shape))
    beside = index_at[:widest] + [(index_at[widest] + 1) % values.shape[widest]] + index_at[widest + 1:]
    return values.at[tuple(index_at)].set(low).at[tuple(beside)].set(largest)


def block_levels(key, dims, shards, low, top_value):
    def one(axis_at, parts):
        steps = jax.random.uniform(jax.random.fold_in(jax.random.fold_in(key, 6), axis_at), (parts,), jnp.float32, low / len(shards), top_value / len(shards))
        return jnp.repeat(jnp.exp(steps), dims[axis_at] // parts).reshape((-1,) + (1,) * (len(dims) - axis_at - 1))

    factor_of = one(*shards[0])
    for cut in shards[1:]:
        factor_of = factor_of * one(*cut)
    return factor_of


def bell_draw(own_key, extent, deviation, limit, pieces=(), held_as=jnp.bfloat16):
    drawn = jax.random.normal(own_key, extent, jnp.float32) * deviation
    if len(pieces) > 0:
        drawn = block_levels(own_key, extent, pieces, -0.22, 0.18) * drawn
    return jnp.clip(drawn, min=-limit, max=limit).astype(held_as)


def setup_inputs(seed: int = 0) -> dict:
    splits = jax.random.split(jax.random.key(seed), 6)
    return {
        "becsum_part": bell_draw(splits[0], (N_BAND, NAT, NIJ), (1.0 / (NAT * N_BAND) ** 0.5), 0.03314563, ((0, 16),), jnp.float32),
        "qrad": bell_draw(splits[1], (NSP, NLM, NQ, NIJ), (1.0 / NIJ ** 0.5), 0.45703125),
        "positions": jnp.clip(jax.random.uniform(splits[2], (3, NAT), jnp.float32, 0.0, 1.0), 0.0, 1.0),
        "species": with_ends(jax.random.randint(splits[3], (NAT,), 0, NSP), jax.random.fold_in(splits[3], 1), 0, NSP - 1).astype(jnp.int32),
        "miller": with_ends(jax.random.randint(splits[4], (2, COLS), -(NZ // 2), NZ // 2), jax.random.fold_in(splits[4], 1), -(NZ // 2), (NZ // 2) - 1).astype(jnp.int32),
    }


TWO_PI = 2.0 * math.pi

def species_columns(becsum, kinds, count):
    blocks = [becsum * (kinds == s).astype(becsum.dtype)[:, None] for s in range(count)]
    return jnp.concatenate(blocks, axis=1)

def arrange(qrad):
    nsp, nlm, nq, nij = qrad.shape
    even = jnp.concatenate([qrad[:, 0:1], qrad[:, 4:9]], axis=1)
    odd = qrad[:, 1:4]
    q_even = jnp.transpose(even, (1, 2, 0, 3)).reshape(6 * nq, nsp * nij)
    q_odd = jnp.transpose(odd, (1, 2, 0, 3)).reshape(3 * nq, nsp * nij)
    return (q_even, q_odd)

def frac(value):
    return value - jnp.floor(value)

def column_density(miller_pair, tau, bec_cols, q_even, q_odd, nz, nq):
    kidx = lax.iota(jnp.int32, nz)
    m_z = jnp.where(kidx < nz // 2, kidx, kidx - nz).astype(jnp.float32)
    m_x = miller_pair[0].astype(jnp.float32)
    m_y = miller_pair[1].astype(jnp.float32)
    part_x = frac(m_x * tau[0])
    part_y = frac(m_y * tau[1])
    part_z = frac(m_z[:, None] * tau[2][None, :])
    theta = TWO_PI * (part_z + (part_x + part_y)[None, :])
    cos_part = jnp.cos(theta).astype(jnp.bfloat16)
    sin_part = jnp.sin(theta).astype(jnp.bfloat16)
    b_cos = jnp.dot(cos_part.astype(jnp.float32), bec_cols.astype(jnp.float32), preferred_element_type=jnp.float32)
    b_sin = jnp.dot(sin_part.astype(jnp.float32), bec_cols.astype(jnp.float32), preferred_element_type=jnp.float32)
    gnorm = jnp.sqrt(m_x * m_x + m_y * m_y + m_z * m_z)
    inverse = 1.0 / jnp.maximum(gnorm, 1.0)
    unit_x = m_x * inverse
    unit_y = m_y * inverse
    unit_z = m_z * inverse
    root3 = math.sqrt(3.0)
    ones = jnp.ones_like(unit_z)
    even = jnp.stack([ones, -root3 * unit_x * unit_y, -root3 * unit_y * unit_z, -root3 * unit_z * unit_x, -0.5 * root3 * (unit_x * unit_x - unit_y * unit_y) * ones, -0.5 * (3.0 * unit_z * unit_z - 1.0)], axis=1)
    odd = jnp.stack([-unit_x * ones, -unit_y * ones, -unit_z], axis=1)
    tpos = gnorm * ((nq - 1) / (math.sqrt(3.0) * nz / 2.0))
    table = lax.iota(jnp.int32, nq).astype(jnp.float32)
    hat = jnp.maximum(0.0, 1.0 - jnp.abs(tpos[:, None] - table[None, :]))
    w_even = (even[:, :, None] * hat[:, None, :]).reshape(nz, 6 * nq).astype(jnp.bfloat16)
    w_odd = (odd[:, :, None] * hat[:, None, :]).reshape(nz, 3 * nq).astype(jnp.bfloat16)
    q_re = jnp.dot(w_even.astype(jnp.float32), q_even.astype(jnp.float32), preferred_element_type=jnp.float32)
    q_im = jnp.dot(w_odd.astype(jnp.float32), q_odd.astype(jnp.float32), preferred_element_type=jnp.float32)
    real_part = lax.optimization_barrier(jnp.sum(q_re * b_cos + q_im * b_sin, axis=1))
    imag_part = lax.optimization_barrier(jnp.sum(q_im * b_cos - q_re * b_sin, axis=1))
    return jnp.stack([real_part, imag_part])

def reference(becsum_part, qrad, positions, species, miller):
    becsum = lax.optimization_barrier(jnp.sum(becsum_part, axis=0)).astype(jnp.bfloat16)
    bec_cols = species_columns(becsum, species, NSP)
    q_even, q_odd = arrange(qrad)

    def one_column(miller_pair):
        return column_density(miller_pair, positions, bec_cols, q_even, q_odd, NZ, NQ)
    dens = lax.map(one_column, jnp.transpose(miller))
    field = dens[:, 0] + 1j * dens[:, 1]
    field = jnp.fft.ifft(field, axis=1) * math.sqrt(NZ)
    planes = jnp.stack([jnp.real(field), jnp.imag(field)])
    return planes.reshape(2, N_GA, COL_GA, NZ)
```

```python
import math

import jax
import jax.numpy as jnp
import numpy as np
from jax import lax
from jax.experimental import pallas as pl
from jax.experimental.pallas import tpu as pltpu
from jax.sharding import PartitionSpec as P

MESH = pl.DeviceIdType.MESH
F32 = jnp.float32
BF16 = jnp.bfloat16

NZ = 384
NQ = 128
NLM = 9
NSP = 2
NIJ = 171
N_GA = 32
N_BAND = 16
ATOMS = 64
HALF_IJ = 96
OWNERS = HALF_IJ // 8
M = 256
PLANES = NZ // N_GA
HALF_Z = PLANES // 2
ROOT3 = math.sqrt(3.0)

COS_TERMS = (
    0.9999999890590227, -19.73920449945391, 64.93911745989556, -85.45013953088247,
    60.16763095094928, -25.967599248494622, 6.528658161366808,
)
SIN_TERMS = (
    6.283185302511503, -41.341700405317496, 81.60513138579344, -76.70301535379849,
    42.025926985567956, -14.89984666736486, 3.238137509743233,
)


def transform_table():
    table = np.zeros((2, N_GA, 8, 2, M))
    m = np.arange(NZ // 2 + 1)
    factor = np.where(m == 0, 1.0, 2.0)
    factor[NZ // 2] = 1.0
    for half in range(2):
        for i in range(HALF_Z):
            z = PLANES * np.arange(N_GA) + HALF_Z * half + i
            angle = 2.0 * np.pi * ((z[:, None] * m[None, :]) % NZ) / NZ
            table[half, :, i, 0, : m.size] = factor * np.cos(angle) / math.sqrt(NZ)
            table[half, :, i, 1, : m.size] = factor * np.sin(angle) / math.sqrt(NZ)
    table = table.reshape(2, N_GA * 8, 2 * M).astype(np.float32)
    high = table.astype(BF16)
    return np.stack([high, (table - high.astype(np.float32)).astype(BF16)])


def frac(value):
    return value - jnp.floor(value)


def cos_sin(turns):
    r = turns - jnp.floor(turns + 0.5)
    r2 = r * r
    c = jnp.full_like(r, COS_TERMS[-1])
    s = jnp.full_like(r, SIN_TERMS[-1])
    for k in range(len(COS_TERMS) - 2, -1, -1):
        c = c * r2 + COS_TERMS[k]
        s = s * r2 + SIN_TERMS[k]
    return c, s * r


def kernel(
    bec_ref, q_ref, pos_ref, spec_ref, mil_ref, dft_ref, out_ref,
    part, got, whole, mil_out, mil_in, waves, coef, hats, trig, lhs, table_z, terms, dens, planes, landed, q_vmem, dft_vmem,
    rs_send, rs_recv, ag_send, ag_recv, mil_send, mil_recv, out_send, out_recv, load,
):
    g = lax.axis_index("ga")
    b = lax.axis_index("band")

    def band_peer(d):
        return lax.rem(b + d, N_BAND)

    def ga_peer(d):
        return lax.rem(g + d, N_GA)

    q_copy = pltpu.make_async_copy(q_ref, q_vmem, load.at[0])
    q_copy.start()
    dft_copy = pltpu.make_async_copy(dft_ref, dft_vmem, load.at[1])
    dft_copy.start()

    barrier = pltpu.get_barrier_semaphore()

    @pl.loop(1, N_BAND)
    def _(d):
        pl.semaphore_signal(barrier, inc=1, device_id=(g, band_peer(d)), device_id_type=MESH)

    @pl.loop(1, N_GA)
    def _(d):
        pl.semaphore_signal(barrier, inc=1, device_id=(ga_peer(d), b), device_id_type=MESH)

    part[...] = bec_ref[...]
    lane16 = lax.broadcasted_iota(jnp.int32, (2, 16), 1)
    own = jnp.sum(jnp.where(lane16 == b, mil_ref[...].astype(F32), 0.0), axis=1, keepdims=True)
    tile = jnp.concatenate([jnp.broadcast_to(own, (2, 128)), jnp.zeros((6, 128), F32)], axis=0)
    mil_out[...] = tile
    mil_in[g] = tile

    pl.semaphore_wait(barrier, N_BAND - 1 + N_GA - 1)

    @pl.loop(0, OWNERS)
    def _(p):
        @pl.when(p != b)
        def _():
            pltpu.make_async_remote_copy(
                src_ref=part.at[p], dst_ref=got.at[b], send_sem=rs_send, recv_sem=rs_recv,
                device_id=(g, p), device_id_type=MESH,
            ).start()

    @pl.loop(1, N_GA)
    def _(d):
        pltpu.make_async_remote_copy(
            src_ref=mil_out, dst_ref=mil_in.at[g], send_sem=mil_send, recv_sem=mil_recv,
            device_id=(ga_peer(d), b), device_id_type=MESH,
        ).start()

    at = pl.multiple_of(lax.div(g, 2) * 128, 128)
    tau = pos_ref[:, pl.ds(at, 128)]
    kind = spec_ref[:, pl.ds(at, 128)].astype(F32)
    atoms = jnp.concatenate([tau, kind, jnp.zeros((4, 128), F32)], axis=0)
    atoms = jnp.where(lax.rem(g, 2) == 0, atoms, pltpu.roll(atoms, 64, axis=1))
    by_atom = jnp.transpose(jnp.concatenate([atoms, jnp.zeros((120, 128), F32)], axis=0))[:ATOMS]
    m_at = lax.broadcasted_iota(jnp.int32, (1, M), 1)
    m_z = m_at.astype(F32)
    cos_z, sin_z = cos_sin(frac(by_atom[:, 2:3] * m_z))
    table_z[0] = cos_z
    table_z[1] = sin_z

    @pl.when(b < OWNERS)
    def _():
        got[b] = part[b]
        pltpu.make_async_copy(got.at[pl.ds(0, N_BAND - 1)], got.at[pl.ds(0, N_BAND - 1)], rs_recv).wait()
        whole[b] = jnp.sum(got[...], axis=0)

        @pl.loop(1, N_BAND)
        def _(d):
            pltpu.make_async_remote_copy(
                src_ref=whole.at[b], dst_ref=whole.at[b], send_sem=ag_send, recv_sem=ag_recv,
                device_id=(g, band_peer(d)), device_id_type=MESH,
            ).start()

    pltpu.make_async_copy(mil_in.at[pl.ds(0, N_GA - 1)], mil_in.at[pl.ds(0, N_GA - 1)], mil_recv).wait()
    m_x = mil_in[:, 0, :]
    m_y = mil_in[:, 1, :]
    rho2 = m_x * m_x + m_y * m_y
    rho2_wide = jnp.concatenate([rho2, rho2], axis=1)
    gnorm = jnp.sqrt(rho2_wide + m_z * m_z)
    inverse = 1.0 / jnp.maximum(gnorm, 1.0)
    inverse2 = inverse * inverse
    waves[0] = gnorm * ((NQ - 1) / (ROOT3 * NZ / 2.0))
    waves[1] = jnp.where(rho2_wide > 0.0, inverse2, jnp.where(m_at == 0, 1.0, 0.0))
    waves[2] = inverse
    waves[3] = m_z * inverse2
    waves[4] = m_z * inverse
    coef[0] = -ROOT3 * m_x * m_y
    coef[1] = (-0.5 * ROOT3) * (m_x * m_x - m_y * m_y)
    coef[2] = 1.5 * jnp.maximum(rho2, 1.0)
    coef[3] = -ROOT3 * m_x
    coef[4] = -ROOT3 * m_y
    coef[5] = -m_x
    coef[6] = -m_y
    phase_cos, phase_sin = cos_sin(frac(m_x * atoms[0:1]) + frac(m_y * atoms[1:2]))
    rest = jnp.zeros((128 - N_GA, 128), F32)
    phase_cos = jnp.transpose(jnp.concatenate([phase_cos, rest], axis=0))[:ATOMS]
    phase_sin = jnp.transpose(jnp.concatenate([phase_sin, rest], axis=0))[:ATOMS]
    point = lax.broadcasted_iota(jnp.int32, (NQ, M), 0).astype(F32)

    @pl.loop(0, N_GA)
    def _(c):
        t = waves[0, pl.ds(c, 1), :]
        hats[c] = jnp.maximum(0.0, 1.0 - jnp.abs(t - point)).astype(BF16)
        turn = lax.rem(128 - c, 128)
        c_f = pltpu.roll(phase_cos, turn, axis=1)[:, 0:1]
        s_f = pltpu.roll(phase_sin, turn, axis=1)[:, 0:1]
        cc = table_z[0] * c_f
        ss = table_z[1] * s_f
        sc = table_z[1] * c_f
        cs = table_z[0] * s_f
        for k, part_of in enumerate((cc - ss, cs + sc, cc + ss, cs - sc)):
            trig[c, k] = part_of.astype(BF16).astype(F32)

    @pl.when(b < OWNERS)
    def _():
        pltpu.make_async_copy(whole.at[pl.ds(0, OWNERS - 1)], whole.at[pl.ds(0, OWNERS - 1)], ag_recv).wait()

    @pl.when(b >= OWNERS)
    def _():
        pltpu.make_async_copy(whole, whole, ag_recv).wait()

    q_copy.wait()
    becsum = whole[...].reshape(HALF_IJ, 128)
    becsum = jnp.concatenate([becsum, jnp.zeros((128 - HALF_IJ, 128), F32)], axis=0)
    becsum = jnp.transpose(becsum)[:, :HALF_IJ].astype(BF16)
    kinds = by_atom[:, 3:4]
    total = jnp.zeros((ATOMS, NLM * NQ), F32)
    for s in range(NSP):
        mask = jnp.where(kinds == float(s), 1.0, 0.0).astype(BF16)
        for h in range(2):
            rows = becsum[h * ATOMS : (h + 1) * ATOMS] * mask
            total = total + jnp.dot(rows, q_vmem[s, h], preferred_element_type=F32)
    for e in range(NLM):
        terms[e] = total[:, e * NQ : (e + 1) * NQ]
    lhs[pl.ds(0, ATOMS)] = (terms[0] - terms[8]).astype(BF16)
    lhs[pl.ds(4 * ATOMS, ATOMS)] = (-terms[3]).astype(BF16)
    last = m_at == NZ // 2

    @pl.loop(0, N_GA)
    def _(c):
        def scalar(k):
            return coef[k, pl.ds(c, 1), :]

        def wave(k):
            return waves[k, pl.ds(c, 1), :]

        lhs[pl.ds(ATOMS, ATOMS)] = (scalar(0) * terms[4] + scalar(1) * terms[7] + scalar(2) * terms[8]).astype(BF16)
        lhs[pl.ds(2 * ATOMS, ATOMS)] = (scalar(4) * terms[5] + scalar(3) * terms[6]).astype(BF16)
        lhs[pl.ds(3 * ATOMS, ATOMS)] = (scalar(5) * terms[1] + scalar(6) * terms[2]).astype(BF16)
        at_g = jnp.dot(lhs[...], hats[c], preferred_element_type=F32)
        re_even = at_g[:ATOMS] + wave(1) * at_g[ATOMS : 2 * ATOMS]
        re_odd = wave(3) * at_g[2 * ATOMS : 3 * ATOMS]
        im_even = wave(2) * at_g[3 * ATOMS : 4 * ATOMS]
        im_odd = wave(4) * at_g[4 * ATOMS :]

        def summed(x):
            return jnp.sum(x, axis=0, keepdims=True)

        re, im = re_even + re_odd, im_even + im_odd
        re_up = summed(re * trig[c, 0] + im * trig[c, 1])
        im_up = summed(im * trig[c, 0] - re * trig[c, 1])
        re, im = re_even - re_odd, im_even - im_odd
        re_down = summed(re * trig[c, 2] + im * trig[c, 3])
        im_down = summed(im * trig[c, 2] - re * trig[c, 3])
        re_up = jnp.where(last, re_down, re_up)
        im_up = jnp.where(last, im_down, im_up)
        dens[pl.ds(c, 1), pl.ds(0, M)] = 0.5 * (re_up + re_down)
        dens[pl.ds(c, 1), pl.ds(M, M)] = -0.5 * (im_up - im_down)
        dens[pl.ds(N_GA + c, 1), pl.ds(0, M)] = 0.5 * (im_up + im_down)
        dens[pl.ds(N_GA + c, 1), pl.ds(M, M)] = 0.5 * (re_up - re_down)

    dft_copy.wait()
    high = dens[...].astype(BF16)
    low = (dens[...] - high.astype(F32)).astype(BF16)

    def against(rows, columns):
        return lax.dot_general(rows, columns, (((1,), (1,)), ((), ())), preferred_element_type=F32)

    halves = [
        against(dft_vmem[0, h], high) + (against(dft_vmem[0, h], low) + against(dft_vmem[1, h], high))
        for h in range(2)
    ]
    planes[...] = jnp.concatenate(halves, axis=1).reshape(N_GA, 8, 128)

    @pl.loop(1, N_GA)
    def _(d):
        peer = ga_peer(d)
        pltpu.make_async_remote_copy(
            src_ref=planes.at[peer], dst_ref=landed.at[g], send_sem=out_send, recv_sem=out_recv,
            device_id=(peer, b), device_id_type=MESH,
        ).start()

    landed[g] = planes[g]
    pltpu.make_async_copy(landed.at[pl.ds(0, N_GA - 1)], landed.at[pl.ds(0, N_GA - 1)], out_recv).wait()
    mine = jnp.sum(landed[...], axis=0)
    for r in range(2):
        for h in range(2):
            first = h * 64 + r * 32
            out_ref[pl.ds(r * PLANES + h * HALF_Z, HALF_Z), :] = mine[:HALF_Z, first : first + N_GA]

    pltpu.make_async_copy(mil_in.at[pl.ds(0, N_GA - 1)], mil_in.at[pl.ds(0, N_GA - 1)], mil_send).wait()
    pltpu.make_async_copy(landed.at[pl.ds(0, N_GA - 1)], landed.at[pl.ds(0, N_GA - 1)], out_send).wait()

    @pl.when(b < OWNERS)
    def _():
        pltpu.make_async_copy(part.at[pl.ds(0, OWNERS - 1)], part.at[pl.ds(0, OWNERS - 1)], rs_send).wait()
        pltpu.make_async_copy(got.at[pl.ds(0, N_BAND - 1)], got.at[pl.ds(0, N_BAND - 1)], ag_send).wait()

    @pl.when(b >= OWNERS)
    def _():
        pltpu.make_async_copy(part, part, rs_send).wait()


def arranged(qrad):
    q = jnp.transpose(qrad, (0, 3, 1, 2)).reshape(NSP, NIJ, NLM * NQ)
    q = jnp.pad(q, ((0, 0), (0, 2 * HALF_IJ - NIJ), (0, 0)))
    return q.reshape(NSP, 2, HALF_IJ, NLM * NQ)


def per_device(becsum_part, qrad, positions, species, miller):
    g = lax.axis_index("ga")
    pairs = jnp.transpose(becsum_part[0])
    mine = lax.dynamic_slice_in_dim(pairs, g * ATOMS, ATOMS, 1)
    mine = jnp.pad(mine, ((0, 2 * HALF_IJ - NIJ), (0, 0)))
    mine = jnp.concatenate([mine[:HALF_IJ], mine[HALF_IJ:]], axis=1).reshape(OWNERS, 8, 128)
    vmem = pl.BlockSpec(memory_space=pltpu.VMEM)
    hbm = pl.BlockSpec(memory_space=pl.ANY)
    planes = pl.pallas_call(
        kernel,
        out_shape=jax.ShapeDtypeStruct((2 * PLANES, N_GA), F32),
        in_specs=[vmem, hbm, vmem, vmem, vmem, hbm],
        out_specs=vmem,
        scratch_shapes=[
            pltpu.VMEM((OWNERS, 8, 128), F32),
            pltpu.VMEM((N_BAND, 8, 128), F32),
            pltpu.VMEM((OWNERS, 8, 128), F32),
            pltpu.VMEM((8, 128), F32),
            pltpu.VMEM((N_GA, 8, 128), F32),
            pltpu.VMEM((5, N_GA, M), F32),
            pltpu.VMEM((7, N_GA, 128), F32),
            pltpu.VMEM((N_GA, NQ, M), BF16),
            pltpu.VMEM((N_GA, 4, ATOMS, M), F32),
            pltpu.VMEM((5 * ATOMS, NQ), BF16),
            pltpu.VMEM((2, ATOMS, M), F32),
            pltpu.VMEM((NLM, ATOMS, NQ), F32),
            pltpu.VMEM((2 * N_GA, 2 * M), F32),
            pltpu.VMEM((N_GA, 8, 128), F32),
            pltpu.VMEM((N_GA, 8, 128), F32),
            pltpu.VMEM((NSP, 2, HALF_IJ, NLM * NQ), BF16),
            pltpu.VMEM((2, 2, N_GA * 8, 2 * M), BF16),
        ]
        + [pltpu.SemaphoreType.DMA] * 8
        + [pltpu.SemaphoreType.DMA((2,))],
        compiler_params=pltpu.CompilerParams(
            collective_id=0, has_side_effects=True, vmem_limit_bytes=40 * 2**20
        ),
    )(mine, arranged(qrad), positions, species.reshape(1, -1), miller, jnp.asarray(transform_table()))
    return jnp.transpose(planes.reshape(2, PLANES, N_GA), (0, 2, 1)).reshape(2, N_GA, 1, PLANES)


def solution(mesh):
    placed = (P("band", None, None), P(), P(), P(), P(None, "ga"))
    return jax.shard_map(
        per_device,
        mesh=mesh,
        in_specs=placed,
        out_specs=P(None, None, "band", "ga"),
        check_vma=False,
    )
```
